32 devices in a mesh: row: 4 (over y, core), col: 4 (over z), depth: 2 (over x).
Axes of the slice: x: 2, y: 2, z: 4, core: 2. Of those that a mesh axis runs over, the one named last changes fastest.
Arguments:
- gate_pre: bfloat16 [256, 26624], P(('col', 'depth'), 'row'), may hold values from -6 to 6
- up_pre: bfloat16 [256, 26624], P(('col', 'depth'), 'row'), may hold values from -6 to 6
- out_grad: bfloat16 [256, 16384], P(('row', 'depth'), 'col'), may hold values from -4 to 4
- down_weight: bfloat16 [26624, 16384], P('row', 'col'), may hold values from -0.0390625 to 0.0390625
Outputs:
- weight_grad: bfloat16 [26624, 16384], P(('row', 'depth'), 'col')
- gate_grad: bfloat16 [256, 26624], P(('col', 'depth'), 'row')
- up_grad: bfloat16 [256, 26624], P(('col', 'depth'), 'row')
The draws below stay inside these ranges and needn't reach their ends.
All inputs are finite; a program needn't handle non-finite values.
Results may differ from the reference program's by a relative error of at most 0.009.
Values may be sent and summed in bfloat16 or wider, within the bound.
No kernel may reach another device: no remote copies, remote signals or barrier semaphores. Data moves between devices by JAX's collectives and lax.ppermute only.
A program may use at most 192 MiB of HBM per device.

```python
import jax
import jax.numpy as jnp
from jax import lax

D = 16384
FF = 26624
TOK_DEV = 32
TOKENS = 256
N_ROW = 4
N_DEPTH = 2


def steps_of(stream_key, dims, pieces, smallest, largest):
    def one(axis_at, shards_of):
        draws = jax.random.uniform(jax.random.fold_in(jax.random.fold_in(stream_key, 6), axis_at), (shards_of,), jnp.float32, smallest / len(pieces), largest / len(pieces))
        return jnp.repeat(jnp.exp(draws), dims[axis_at] // shards_of).reshape((-1,) + (1,) * (len(dims) - axis_at - 1))

    loudness = one(*pieces[0])
    for cut in pieces[1:]:
        loudness = loudness * one(*cut)
    return loudness


def centred(own_key, extent, spread, bound, pieces=(), held_as=jnp.bfloat16):
    entries = spread * jax.random.normal(own_key, extent, jnp.float32)
    if pieces:
        entries = entries * steps_of(own_key, extent, pieces, -0.22, 0.18)
    return jnp.clip(entries, -bound, bound).astype(held_as)


def setup_inputs(seed: int = 0) -> dict:
    arg_keys = jax.random.split(jax.random.key(seed), 5)
    return {
        "gate_pre": centred(arg_keys[0], (TOKENS, FF), 1.5, 6.0, ((0, 8), (1, 4))),
        "up_pre": centred(arg_keys[1], (TOKENS, FF), 1.0, 6.0, ((0, 8), (1, 4))),
        "out_grad": centred(arg_keys[2], (TOKENS, D), (TOKENS ** -0.25), 4.0, ((0, 8), (1, 4))),
        "down_weight": centred(arg_keys[3], (FF, D), FF ** -0.5, 0.0390625, ((0, 4), (1, 4))),
    }


def reference(gate_pre, up_pre, out_grad, down_weight):
    gate_vals = gate_pre.astype(jnp.float32)
    up_vals = up_pre.astype(jnp.float32)
    sigma_gate = jax.nn.sigmoid(gate_vals)
    act = gate_vals * sigma_gate
    hidden = (act * up_vals).astype(jnp.bfloat16)
    hidden_grad = lax.dot_general(out_grad, down_weight, (((1,), (1,)), ((), ())), preferred_element_type=jnp.float32)
    up_grad = (hidden_grad * act).astype(jnp.bfloat16)
    gate_grad = (hidden_grad * up_vals * sigma_gate * (1.0 + gate_vals * (1.0 - sigma_gate))).astype(jnp.bfloat16)
    hidden_blocks = hidden.reshape(N_ROW, N_DEPTH, TOK_DEV, FF)
    grad_blocks = out_grad.reshape(N_ROW, N_DEPTH, TOK_DEV, D)

    def add_layer(total, layer):
        rows_hidden = lax.dynamic_index_in_dim(hidden_blocks, layer, 1, keepdims=False).reshape(N_ROW * TOK_DEV, FF)
        rows_grad = lax.dynamic_index_in_dim(grad_blocks, layer, 1, keepdims=False).reshape(N_ROW * TOK_DEV, D)
        partial_sum = lax.dot_general(rows_hidden, rows_grad, (((0,), (0,)), ((), ())), preferred_element_type=jnp.float32)
        rounded = lax.optimization_barrier(partial_sum.astype(jnp.bfloat16))
        return total + rounded.astype(jnp.float32), None

    total, unused = lax.scan(add_layer, jnp.zeros((FF, D), jnp.float32), jnp.arange(N_DEPTH, dtype=jnp.int32))
    weight_grad = total.astype(jnp.bfloat16)
    return weight_grad, gate_grad, up_grad
```

```python
import functools

import jax
import jax.numpy as jnp
from jax import lax
from jax.experimental import pallas as pl
from jax.experimental.pallas import tpu as pltpu
from jax.sharding import PartitionSpec as P

BF16 = jnp.bfloat16
QUICK = pl.CostEstimate(flops=1, bytes_accessed=1, transcendentals=0)
F32 = jnp.float32


def xor_pairs(size, distance):
    return [(i, i ^ distance) for i in range(size)]


def block_copies(shift, refs, scratch, base, tok, sems):
    copies = []
    for i, (value, ref) in enumerate(zip((0, 2, 1, 3), refs)):
        start = pl.multiple_of(base + jnp.bitwise_xor(shift, value) * tok, tok)
        copies.append(
            pltpu.make_async_copy(ref, scratch.at[pl.ds(start, tok)], sems.at[i])
        )
    return copies


def hidden_kernel(depth_ref, gate_ref, up_ref, mine, theirs):
    half = mine.shape[1]
    for ref, at in ((mine, depth_ref[0]), (theirs, 1 - depth_ref[0])):
        columns = pl.ds(pl.multiple_of(at * half, 128), half)
        gate = gate_ref[:, columns].astype(F32)
        up = up_ref[:, columns].astype(F32)
        ref[...] = (gate * jax.nn.sigmoid(gate) * up).astype(ref.dtype)


def hidden_halves(depth, gate_pre, up_pre):
    tok, ff = gate_pre.shape
    vmem = pl.BlockSpec(memory_space=pltpu.VMEM)
    return pl.pallas_call(
        hidden_kernel,
        out_shape=[jax.ShapeDtypeStruct((tok, ff // 2), BF16)] * 2,
        in_specs=[pl.BlockSpec(memory_space=pltpu.SMEM), vmem, vmem],
        out_specs=[vmem, vmem],
        compiler_params=pltpu.CompilerParams(vmem_limit_bytes=8 << 20),
        cost_estimate=QUICK,
    )(depth, gate_pre, up_pre)


def cuts(rows, most):
    parts = -(-rows // most)
    step = -(-rows // parts // 128) * 128
    return [(at, min(step, rows - at)) for at in range(0, rows, step)]


def in_hbm(arrays):
    return [pltpu.with_memory_space_constraint(x, pltpu.HBM) for x in arrays]


ANYWHERE = pl.BlockSpec(memory_space=pl.ANY)
VMEM = pl.BlockSpec(memory_space=pltpu.VMEM)
SMEM = pl.BlockSpec(memory_space=pltpu.SMEM)


def partial_kernel(tok, first, tiles, n_after, shift_ref, *refs):
    grads_in, w_ref, refs = refs[:4], refs[4], refs[5 + n_after :]
    terms_out, (grads, rows, sems, w_sems) = refs[:4], refs[4:]
    copies = block_copies(shift_ref[0], grads_in, grads, 0, tok, sems)
    fetches = [
        pltpu.make_async_copy(
            w_ref.at[pl.ds(first + at, size)], rows.at[pl.ds(at, size)], w_sems.at[i]
        )
        for i, (at, size) in enumerate(tiles)
    ]
    for copy in copies:
        copy.start()
    for copy in copies:
        copy.wait()
    for fetch in fetches:
        fetch.start()
    for fetch, (at, size) in zip(fetches, tiles):
        fetch.wait()
        terms = lax.dot_general(
            grads[...],
            rows[at : at + size, :],
            (((1,), (1,)), ((), ())),
            preferred_element_type=F32,
        )
        for k, ref in enumerate(terms_out):
            ref[:, at : at + size] = terms[k * tok : (k + 1) * tok].astype(ref.dtype)


def partials(shift, grads, weight, first, rows, after):
    tok, width = grads[0].shape
    tiles = [(0, 256)] + [(256 + at, size) for at, size in cuts(rows - 256, 512)]
    return pl.pallas_call(
        functools.partial(partial_kernel, tok, first, tiles, len(after)),
        out_shape=[jax.ShapeDtypeStruct((tok, rows), F32)]
        + [jax.ShapeDtypeStruct((tok, rows), BF16)] * 3,
        in_specs=[SMEM] + [ANYWHERE] * (5 + len(after)),
        out_specs=[VMEM] * 4,
        scratch_shapes=[
            pltpu.VMEM((4 * tok, width), BF16),
            pltpu.VMEM((rows, width), BF16),
            pltpu.SemaphoreType.DMA((4,)),
            pltpu.SemaphoreType.DMA((len(tiles),)),
        ],
        compiler_params=pltpu.CompilerParams(vmem_limit_bytes=40 << 20),
        cost_estimate=QUICK,
    )(shift, *in_hbm([*grads, weight, *after]))


def outer_kernel(tok, tile, shift_ref, *refs):
    out_ref, token, grads, hidden, ready, sems, in_sems = refs[16:]
    token[...] = jnp.zeros_like(token)
    copies = []
    for half in range(2):
        base = 4 * tok * half
        copies += block_copies(
            shift_ref[0], refs[4 * half : 4 * half + 4], grads, base, tok, in_sems.at[half]
        )
        for k, ref in zip((0, 2, 1, 3), refs[8 + 4 * half : 12 + 4 * half]):
            rows = pl.ds(base + k * tok, tok)
            copies.append(
                pltpu.make_async_copy(ref, hidden.at[rows], in_sems.at[half, 4 + k])
            )
    for copy in copies:
        copy.start()
    for copy in copies:
        copy.wait()
    steps = hidden.shape[1] // tile
    slots = ready.shape[0]

    def copy_out(i):
        return pltpu.make_async_copy(
            ready.at[i % slots], out_ref.at[pl.ds(i * tile, tile)], sems.at[i % slots]
        )

    for i in range(steps):
        if i >= slots:
            copy_out(i - slots).wait()
        ready[i % slots] = lax.dot_general(
            hidden[:, i * tile : (i + 1) * tile],
            grads[...],
            (((0,), (0,)), ((), ())),
            preferred_element_type=F32,
        ).astype(BF16)
        copy_out(i).start()
    for i in range(steps - slots, steps):
        copy_out(i).wait()


def outer(shift, grads, hidden, tile=128, slots=26):
    tok, width = grads[0].shape
    rows = hidden[0].shape[1]
    return pl.pallas_call(
        functools.partial(outer_kernel, tok, tile),
        out_shape=[
            jax.ShapeDtypeStruct((rows, width), BF16),
            jax.ShapeDtypeStruct((8, 128), F32),
        ],
        in_specs=[SMEM] + [ANYWHERE] * 16,
        out_specs=[ANYWHERE, VMEM],
        scratch_shapes=[
            pltpu.VMEM((8 * tok, width), BF16),
            pltpu.VMEM((8 * tok, rows), BF16),
            pltpu.VMEM((slots, tile, width), BF16),
            pltpu.SemaphoreType.DMA((slots,)),
            pltpu.SemaphoreType.DMA((2, 8)),
        ],
        compiler_params=pltpu.CompilerParams(vmem_limit_bytes=40 << 20),
        cost_estimate=QUICK,
    )(shift, *in_hbm(grads), *in_hbm(hidden))


def finish(hidden_grad, gate_vals, up_vals):
    sigma_gate = jax.nn.sigmoid(gate_vals)
    up_grad = (hidden_grad * (gate_vals * sigma_gate)).astype(BF16)
    gate_grad = (
        hidden_grad * up_vals * sigma_gate * (1.0 + gate_vals * (1.0 - sigma_gate))
    ).astype(BF16)
    return gate_grad, up_grad


def finish_kernel(parts, gate_ref, up_ref, *refs):
    gate_out, up_out = refs[-2:]
    at = 0
    for i in range(parts):
        p0, r1, r2, r3 = refs[4 * i : 4 * i + 4]
        columns = slice(at, at + p0.shape[1])
        total = p0[...] + r1[...].astype(F32) + r2[...].astype(F32) + r3[...].astype(F32)
        gate_out[:, columns], up_out[:, columns] = finish(
            total, gate_ref[:, columns].astype(F32), up_ref[:, columns].astype(F32)
        )
        at += p0.shape[1]


def finished(gate_pre, up_pre, sums, after):
    vmem = pl.BlockSpec(memory_space=pltpu.VMEM)
    terms = [term for part in sums for term in part]
    return pl.pallas_call(
        functools.partial(finish_kernel, len(sums)),
        out_shape=[jax.ShapeDtypeStruct(gate_pre.shape, BF16)] * 2,
        in_specs=[vmem] * (2 + len(terms)) + [pl.BlockSpec(memory_space=pl.ANY)],
        out_specs=[vmem, vmem],
        compiler_params=pltpu.CompilerParams(vmem_limit_bytes=16 << 20),
    )(gate_pre, up_pre, *terms, after)


def by_distance(gate_pre, up_pre, out_grad, down_weight):
    ff = gate_pre.shape[1]
    half = ff // 2
    row, col, depth = (lax.axis_index(a) for a in ("row", "col", "depth"))
    shift = jnp.bitwise_xor(row, col).astype(jnp.int32).reshape(1)

    def send(x, axis, distance):
        return lax.ppermute(x, axis, xor_pairs(lax.axis_size(axis), distance))

    g0 = out_grad
    g2 = send(g0, "row", 2)
    g1 = send(g0, "row", 1)
    g3 = send(g2, "row", 1)

    mine, theirs = hidden_halves(depth.astype(jnp.int32).reshape(1), gate_pre, up_pre)
    other = send(theirs, "depth", 1)

    def gather_col(x):
        x2 = send(x, "col", 2)
        return x, x2, send(x, "col", 1), send(x2, "col", 1)

    own_layer = gather_col(mine)
    other_layer = gather_col(other)

    q0 = send(g0, "depth", 1)
    q2 = send(q0, "row", 2)
    q1 = send(q0, "row", 1)
    q3 = send(q2, "row", 1)

    grads = (g0, g2, g1, g3)
    def reduced(terms):
        p0, p1, p2, p3 = terms
        r2, r3, r1 = send(p2, "col", 2), send(p3, "col", 3), send(p1, "col", 1)
        return p0, r1, r2, r3

    after = (own_layer[1], q0)
    sums = [reduced(partials(shift, grads, down_weight, 0, half, after))]
    after = (own_layer[2], other_layer[1], other_layer[2], q2)
    sums.append(reduced(partials(shift, grads, down_weight, half, ff - half, after)))
    weight_grad, token = outer(shift, grads + (q0, q2, q1, q3), own_layer + other_layer)
    gate_grad, up_grad = finished(gate_pre, up_pre, sums, token)
    return weight_grad, gate_grad, up_grad


def by_collectives(gate_pre, up_pre, out_grad, down_weight):
    tok, ff = gate_pre.shape
    n_row, n_depth = lax.axis_size("row"), lax.axis_size("depth")
    gate_vals = gate_pre.astype(F32)
    up_vals = up_pre.astype(F32)
    hidden = (gate_vals * jax.nn.sigmoid(gate_vals) * up_vals).astype(BF16)
    layers = lax.all_to_all(hidden, "depth", split_axis=1, concat_axis=0, tiled=True)
    hidden_all = lax.all_gather(layers, "col", axis=0, tiled=True)
    grads_all = lax.all_gather(out_grad, ("row", "depth"), axis=0, tiled=True)
    weight_grad = lax.dot_general(
        hidden_all, grads_all, (((0,), (0,)), ((), ())), preferred_element_type=F32
    ).astype(BF16)
    layer = lax.dynamic_index_in_dim(
        grads_all.reshape(n_row, n_depth, tok, -1), lax.axis_index("depth"), 1, False
    ).reshape(n_row * tok, -1)
    hidden_terms = lax.dot_general(
        layer, down_weight, (((1,), (1,)), ((), ())), preferred_element_type=F32
    )
    hidden_grad = lax.psum_scatter(hidden_terms, "col", scatter_dimension=0, tiled=True)
    gate_grad, up_grad = finish(hidden_grad, gate_vals, up_vals)
    return weight_grad, gate_grad, up_grad


def solution(mesh):
    sizes = tuple(mesh.shape[a] for a in ("row", "col", "depth"))
    placed = (
        P(("col", "depth"), "row"),
        P(("col", "depth"), "row"),
        P(("row", "depth"), "col"),
        P("row", "col"),
    )
    return jax.shard_map(
        by_distance if sizes == (4, 4, 2) else by_collectives,
        mesh=mesh,
        in_specs=placed,
        out_specs=(
            P(("row", "depth"), "col"),
            P(("col", "depth"), "row"),
            P(("col", "depth"), "row"),
        ),
        check_vma=False,
    )
```

```python
import functools

import jax
import jax.numpy as jnp
from jax import lax
from jax.experimental import pallas as pl
from jax.experimental.pallas import tpu as pltpu
from jax.sharding import PartitionSpec as P

BF16 = jnp.bfloat16
QUICK = pl.CostEstimate(flops=1, bytes_accessed=1, transcendentals=0)
F32 = jnp.float32


def xor_pairs(size, distance):
    return [(i, i ^ distance) for i in range(size)]


def block_copies(shift, refs, scratch, base, tok, sems):
    copies = []
    for i, (value, ref) in enumerate(zip((0, 2, 1, 3), refs)):
        start = pl.multiple_of(base + jnp.bitwise_xor(shift, value) * tok, tok)
        copies.append(
            pltpu.make_async_copy(ref, scratch.at[pl.ds(start, tok)], sems.at[i])
        )
    return copies


def hidden_kernel(depth_ref, gate_ref, up_ref, mine, theirs):
    half = mine.shape[1]
    for ref, at in ((mine, depth_ref[0]), (theirs, 1 - depth_ref[0])):
        columns = pl.ds(pl.multiple_of(at * half, 128), half)
        gate = gate_ref[:, columns].astype(F32)
        up = up_ref[:, columns].astype(F32)
        ref[...] = (gate * jax.nn.sigmoid(gate) * up).astype(ref.dtype)


def hidden_halves(depth, gate_pre, up_pre):
    tok, ff = gate_pre.shape
    vmem = pl.BlockSpec(memory_space=pltpu.VMEM)
    return pl.pallas_call(
        hidden_kernel,
        out_shape=[jax.ShapeDtypeStruct((tok, ff // 2), BF16)] * 2,
        in_specs=[pl.BlockSpec(memory_space=pltpu.SMEM), vmem, vmem],
        out_specs=[vmem, vmem],
        compiler_params=pltpu.CompilerParams(vmem_limit_bytes=8 << 20),
        cost_estimate=QUICK,
    )(depth, gate_pre, up_pre)


def cuts(rows, most):
    parts = -(-rows // most)
    step = -(-rows // parts // 128) * 128
    return [(at, min(step, rows - at)) for at in range(0, rows, step)]


def in_hbm(arrays):
    return [pltpu.with_memory_space_constraint(x, pltpu.HBM) for x in arrays]


ANYWHERE = pl.BlockSpec(memory_space=pl.ANY)
VMEM = pl.BlockSpec(memory_space=pltpu.VMEM)
SMEM = pl.BlockSpec(memory_space=pltpu.SMEM)


def partial_kernel(tok, first, tiles, n_after, shift_ref, *refs):
    grads_in, w_ref, refs = refs[:4], refs[4], refs[5 + n_after :]
    terms_out, (grads, rows, sems, w_sems) = refs[:4], refs[4:]
    copies = block_copies(shift_ref[0], grads_in, grads, 0, tok, sems)
    fetches = [
        pltpu.make_async_copy(
            w_ref.at[pl.ds(first + at, size)], rows.at[pl.ds(at, size)], w_sems.at[i]
        )
        for i, (at, size) in enumerate(tiles)
    ]
    for copy in copies:
        copy.start()
    for copy in copies:
        copy.wait()
    for fetch in fetches:
        fetch.start()
    for fetch, (at, size) in zip(fetches, tiles):
        fetch.wait()
        terms = lax.dot_general(
            grads[...],
            rows[at : at + size, :],
            (((1,), (1,)), ((), ())),
            preferred_element_type=F32,
        )
        for k, ref in enumerate(terms_out):
            ref[:, at : at + size] = terms[k * tok : (k + 1) * tok].astype(ref.dtype)


def partials(shift, grads, weight, first, rows, after):
    tok, width = grads[0].shape
    tiles = [(0, 256)] + [(256 + at, size) for at, size in cuts(rows - 256, 512)]
    return pl.pallas_call(
        functools.partial(partial_kernel, tok, first, tiles, len(after)),
        out_shape=[jax.ShapeDtypeStruct((tok, rows), F32)]
        + [jax.ShapeDtypeStruct((tok, rows), BF16)] * 3,
        in_specs=[SMEM] + [ANYWHERE] * (5 + len(after)),
        out_specs=[VMEM] * 4,
        scratch_shapes=[
            pltpu.VMEM((4 * tok, width), BF16),
            pltpu.VMEM((rows, width), BF16),
            pltpu.SemaphoreType.DMA((4,)),
            pltpu.SemaphoreType.DMA((len(tiles),)),
        ],
        compiler_params=pltpu.CompilerParams(vmem_limit_bytes=40 << 20),
        cost_estimate=QUICK,
    )(shift, *in_hbm([*grads, weight, *after]))


def outer_kernel(tok, tile, shift_ref, *refs):
    out_ref, token, grads, hidden, ready, sems, in_sems = refs[17:]
    token[...] = jnp.zeros_like(token)
    copies = []
    for half in range(2):
        base = 4 * tok * half
        copies += block_copies(
            shift_ref[0], refs[4 * half : 4 * half + 4], grads, base, tok, in_sems.at[half]
        )
        for k, ref in zip((0, 2, 1, 3), refs[8 + 4 * half : 12 + 4 * half]):
            rows = pl.ds(base + k * tok, tok)
            copies.append(
                pltpu.make_async_copy(ref, hidden.at[rows], in_sems.at[half, 4 + k])
            )
    for copy in copies:
        copy.start()
    for copy in copies:
        copy.wait()
    steps = hidden.shape[1] // tile
    slots = ready.shape[0]

    def copy_out(i):
        return pltpu.make_async_copy(
            ready.at[i % slots], out_ref.at[pl.ds(i * tile, tile)], sems.at[i % slots]
        )

    for i in range(steps):
        if i >= slots:
            copy_out(i - slots).wait()
        ready[i % slots] = lax.dot_general(
            hidden[:, i * tile : (i + 1) * tile],
            grads[...],
            (((0,), (0,)), ((), ())),
            preferred_element_type=F32,
        ).astype(BF16)
        copy_out(i).start()
    for i in range(steps - slots, steps):
        copy_out(i).wait()


def outer(shift, grads, hidden, after, tile=128, slots=26):
    tok, width = grads[0].shape
    rows = hidden[0].shape[1]
    return pl.pallas_call(
        functools.partial(outer_kernel, tok, tile),
        out_shape=[
            jax.ShapeDtypeStruct((rows, width), BF16),
            jax.ShapeDtypeStruct((8, 128), F32),
        ],
        in_specs=[SMEM] + [ANYWHERE] * 17,
        out_specs=[ANYWHERE, VMEM],
        scratch_shapes=[
            pltpu.VMEM((8 * tok, width), BF16),
            pltpu.VMEM((8 * tok, rows), BF16),
            pltpu.VMEM((slots, tile, width), BF16),
            pltpu.SemaphoreType.DMA((slots,)),
            pltpu.SemaphoreType.DMA((2, 8)),
        ],
        compiler_params=pltpu.CompilerParams(vmem_limit_bytes=40 << 20),
        cost_estimate=QUICK,
    )(shift, *in_hbm([*grads, *hidden]), after)


def finish(hidden_grad, gate_vals, up_vals):
    sigma_gate = jax.nn.sigmoid(gate_vals)
    up_grad = (hidden_grad * (gate_vals * sigma_gate)).astype(BF16)
    gate_grad = (
        hidden_grad * up_vals * sigma_gate * (1.0 + gate_vals * (1.0 - sigma_gate))
    ).astype(BF16)
    return gate_grad, up_grad


def finish_kernel(gate_ref, up_ref, p0, r1, r2, r3, *refs):
    gate_out, up_out, token = refs[-3:]
    total = p0[...] + r1[...].astype(F32) + r2[...].astype(F32) + r3[...].astype(F32)
    gate_out[...], up_out[...] = finish(
        total, gate_ref[...].astype(F32), up_ref[...].astype(F32)
    )
    token[...] = jnp.zeros_like(token)


def finished(gate_pre, up_pre, part, terms, others):
    tok, width = terms[0].shape
    here = pl.BlockSpec((tok, width), lambda i: (0, part))
    term = pl.BlockSpec((tok, width), lambda i: (0, 0))
    return pl.pallas_call(
        finish_kernel,
        grid=(1,),
        out_shape=[jax.ShapeDtypeStruct(gate_pre.shape, BF16)] * 2
        + [jax.ShapeDtypeStruct((8, 128), F32)],
        in_specs=[here, here] + [term] * 4 + [ANYWHERE] * len(others),
        out_specs=[here, here, pl.BlockSpec((8, 128), lambda i: (0, 0))],
        input_output_aliases={6: 0, 7: 1} if part else {},
        compiler_params=pltpu.CompilerParams(vmem_limit_bytes=16 << 20),
        cost_estimate=QUICK,
    )(gate_pre, up_pre, *terms, *others)


def by_distance(gate_pre, up_pre, out_grad, down_weight):
    ff = gate_pre.shape[1]
    half = ff // 2
    row, col, depth = (lax.axis_index(a) for a in ("row", "col", "depth"))
    shift = jnp.bitwise_xor(row, col).astype(jnp.int32).reshape(1)

    def send(x, axis, distance):
        return lax.ppermute(x, axis, xor_pairs(lax.axis_size(axis), distance))

    g0 = out_grad
    g2 = send(g0, "row", 2)
    g1 = send(g0, "row", 1)
    g3 = send(g2, "row", 1)

    mine, theirs = hidden_halves(depth.astype(jnp.int32).reshape(1), gate_pre, up_pre)
    other = send(theirs, "depth", 1)

    def gather_col(x):
        x2 = send(x, "col", 2)
        return x, x2, send(x, "col", 1), send(x2, "col", 1)

    own_layer = gather_col(mine)
    other_layer = gather_col(other)

    q0 = send(g0, "depth", 1)
    q2 = send(q0, "row", 2)
    q1 = send(q0, "row", 1)
    q3 = send(q2, "row", 1)

    grads = (g0, g2, g1, g3)
    def reduced(terms):
        p0, p1, p2, p3 = terms
        r2, r3, r1 = send(p2, "col", 2), send(p3, "col", 3), send(p1, "col", 1)
        return p0, r1, r2, r3

    terms = partials(shift, grads, down_weight, 0, half, (other,))
    first = reduced(terms)
    second = reduced(partials(shift, grads, down_weight, half, half, (terms[0], *own_layer[1:3], *other_layer[1:3], q0)))
    gate_grad, up_grad, token = finished(gate_pre, up_pre, 0, first, ())
    weight_grad, token = outer(
        shift,
        (g0, g2, g1, g3, q0, q2, q1, q3),
        own_layer + other_layer,
        token,
    )
    gate_grad, up_grad, _ = finished(
        gate_pre, up_pre, 1, second, (gate_grad, up_grad, token)
    )
    return weight_grad, gate_grad, up_grad


def by_collectives(gate_pre, up_pre, out_grad, down_weight):
    tok, ff = gate_pre.shape
    n_row, n_depth = lax.axis_size("row"), lax.axis_size("depth")
    gate_vals = gate_pre.astype(F32)
    up_vals = up_pre.astype(F32)
    hidden = (gate_vals * jax.nn.sigmoid(gate_vals) * up_vals).astype(BF16)
    layers = lax.all_to_all(hidden, "depth", split_axis=1, concat_axis=0, tiled=True)
    hidden_all = lax.all_gather(layers, "col", axis=0, tiled=True)
    grads_all = lax.all_gather(out_grad, ("row", "depth"), axis=0, tiled=True)
    weight_grad = lax.dot_general(
        hidden_all, grads_all, (((0,), (0,)), ((), ())), preferred_element_type=F32
    ).astype(BF16)
    layer = lax.dynamic_index_in_dim(
        grads_all.reshape(n_row, n_depth, tok, -1), lax.axis_index("depth"), 1, False
    ).reshape(n_row * tok, -1)
    hidden_terms = lax.dot_general(
        layer, down_weight, (((1,), (1,)), ((), ())), preferred_element_type=F32
    )
    hidden_grad = lax.psum_scatter(hidden_terms, "col", scatter_dimension=0, tiled=True)
    gate_grad, up_grad = finish(hidden_grad, gate_vals, up_vals)
    return weight_grad, gate_grad, up_grad


def solution(mesh):
    sizes = tuple(mesh.shape[a] for a in ("row", "col", "depth"))
    placed = (
        P(("col", "depth"), "row"),
        P(("col", "depth"), "row"),
        P(("row", "depth"), "col"),
        P("row", "col"),
    )
    return jax.shard_map(
        by_distance if sizes == (4, 4, 2) else by_collectives,
        mesh=mesh,
        in_specs=placed,
        out_specs=(
            P(("row", "depth"), "col"),
            P(("col", "depth"), "row"),
            P(("col", "depth"), "row"),
        ),
        check_vma=False,
    )
```

```python
import functools

import jax
import jax.numpy as jnp
from jax import lax
from jax.experimental import pallas as pl
from jax.experimental.pallas import tpu as pltpu
from jax.sharding import PartitionSpec as P

BF16 = jnp.bfloat16
QUICK = pl.CostEstimate(flops=1, bytes_accessed=1, transcendentals=0)
F32 = jnp.float32


def of_bytes(n):
    return pl.CostEstimate(flops=1, bytes_accessed=n, transcendentals=0)


def xor_pairs(size, distance):
    return [(i, i ^ distance) for i in range(size)]


def block_copies(shift, pairs, scratch, base, sems):
    tok = pairs[0].shape[0] // 2
    copies = []
    for value in range(4):
        ref = pairs[value % 2].at[pl.ds(value // 2 * tok, tok)]
        start = pl.multiple_of(base + jnp.bitwise_xor(shift, value) * tok, tok)
        copies.append(
            pltpu.make_async_copy(ref, scratch.at[pl.ds(start, tok)], sems.at[value])
        )
    return copies


def in_hbm(arrays):
    return [pltpu.with_memory_space_constraint(x, pltpu.HBM) for x in arrays]


ANYWHERE = pl.BlockSpec(memory_space=pl.ANY)
VMEM = pl.BlockSpec(memory_space=pltpu.VMEM)
SMEM = pl.BlockSpec(memory_space=pltpu.SMEM)


def hidden_kernel(
    depth_ref, gate_ref, up_ref, og_ref, mine, theirs, og_out, gates, ups, sems, og_sem
):
    half = mine.shape[1]
    copies = []
    for i, at in enumerate((1 - depth_ref[0], depth_ref[0])):
        columns = pl.ds(pl.multiple_of(at * half, 128), half)
        for j, (src, dst) in enumerate(((gate_ref, gates), (up_ref, ups))):
            copies.append(
                pltpu.make_async_copy(src.at[:, columns], dst.at[i], sems.at[i, j])
            )
    passed = pltpu.make_async_copy(og_ref, og_out, og_sem)
    for copy in copies + [passed]:
        copy.start()
    for i, out in enumerate((theirs, mine)):
        copies[2 * i].wait()
        copies[2 * i + 1].wait()
        gate = gates[i].astype(F32)
        out[...] = (gate * jax.nn.sigmoid(gate) * ups[i].astype(F32)).astype(out.dtype)
    passed.wait()


def hidden_halves(depth, gate_pre, up_pre, out_grad):
    tok, ff = gate_pre.shape
    return pl.pallas_call(
        hidden_kernel,
        out_shape=[jax.ShapeDtypeStruct((tok, ff // 2), BF16)] * 2
        + [jax.ShapeDtypeStruct(out_grad.shape, BF16)],
        in_specs=[SMEM] + [ANYWHERE] * 3,
        out_specs=[VMEM, VMEM, VMEM],
        scratch_shapes=[pltpu.VMEM((2, tok, ff // 2), BF16)] * 2
        + [pltpu.SemaphoreType.DMA((2, 2)), pltpu.SemaphoreType.DMA],
        compiler_params=pltpu.CompilerParams(vmem_limit_bytes=16 << 20),
        cost_estimate=QUICK,
    )(depth, *in_hbm([gate_pre, up_pre, out_grad]))


def cuts(rows, most):
    parts = -(-rows // most)
    step = -(-rows // parts // 128) * 128
    return [(at, min(step, rows - at)) for at in range(0, rows, step)]


def stack_kernel(*refs):
    ins, outs, sems = refs[:4], refs[4:6], refs[6]
    tok = ins[0].shape[0]
    copies = [
        pltpu.make_async_copy(
            ref, outs[i // 2].at[pl.ds(i % 2 * tok, tok)], sems.at[i]
        )
        for i, ref in enumerate(ins)
    ]
    for copy in copies:
        copy.start()
    for copy in copies:
        copy.wait()


def stacked(g0, g2, mine, other):
    tok = g0.shape[0]
    return pl.pallas_call(
        stack_kernel,
        out_shape=[
            jax.ShapeDtypeStruct((2 * tok, g0.shape[1]), BF16),
            jax.ShapeDtypeStruct((2 * tok, mine.shape[1]), BF16),
        ],
        in_specs=[ANYWHERE] * 4,
        out_specs=[VMEM] * 2,
        scratch_shapes=[pltpu.SemaphoreType.DMA((4,))],
        cost_estimate=QUICK,
    )(*in_hbm([g0, g2, mine, other]))


def partial_kernel(tok, first, tiles, shift_ref, pair, cores, w_ref, *refs):
    terms_out, (grads, rows, sems, w_sems) = refs[:4], refs[4:]
    fetches = [
        pltpu.make_async_copy(
            w_ref.at[pl.ds(first + at, size)], rows.at[pl.ds(at, size)], w_sems.at[i]
        )
        for i, (at, size) in enumerate(tiles)
    ]
    copies = block_copies(shift_ref[0], (pair, cores), grads, 0, sems)
    for copy in copies + fetches[:1]:
        copy.start()
    for copy in copies:
        copy.wait()
    for fetch in fetches[1:]:
        fetch.start()
    for fetch, (at, size) in zip(fetches, tiles):
        fetch.wait()
        terms = lax.dot_general(
            grads[...],
            rows[at : at + size, :],
            (((1,), (1,)), ((), ())),
            preferred_element_type=F32,
        )
        for k, ref in enumerate(terms_out):
            ref[:, at : at + size] = terms[k * tok : (k + 1) * tok].astype(ref.dtype)


def partials(shift, pairs, weight, first, rows):
    tok, width = pairs[0].shape[0] // 2, pairs[0].shape[1]
    tiles = [(0, 256)] + [(256 + at, size) for at, size in cuts(rows - 256, 512)]
    return pl.pallas_call(
        functools.partial(partial_kernel, tok, first, tiles),
        out_shape=[jax.ShapeDtypeStruct((tok, rows), F32)]
        + [jax.ShapeDtypeStruct((tok, rows), BF16)] * 3,
        in_specs=[SMEM] + [ANYWHERE] * 3,
        out_specs=[VMEM] * 4,
        scratch_shapes=[
            pltpu.VMEM((4 * tok, width), BF16),
            pltpu.VMEM((rows, width), BF16),
            pltpu.SemaphoreType.DMA((4,)),
            pltpu.SemaphoreType.DMA((len(tiles),)),
        ],
        compiler_params=pltpu.CompilerParams(vmem_limit_bytes=40 << 20),
        cost_estimate=of_bytes(2 * rows * width),
    )(shift, *pairs, *in_hbm([weight]))


def outer_kernel(tok, tile, shift_ref, *refs):
    out_ref, token, grads, hidden, ready, sems, in_sems = refs[8:]
    token[...] = jnp.zeros_like(token)
    copies = []
    for half in range(2):
        pairs = refs[2 * half : 2 * half + 2]
        copies += block_copies(
            shift_ref[0], pairs, grads, 4 * half * tok, in_sems.at[half]
        )
    for half in range(2):
        for k, ref in zip((0, 2, 1, 3), refs[4:8]):
            copies.append(
                pltpu.make_async_copy(
                    ref.at[pl.ds(half * tok, tok)],
                    hidden.at[pl.ds((4 * half + k) * tok, tok)],
                    in_sems.at[half, 4 + k],
                )
            )
    for copy in copies:
        copy.start()
    for copy in copies:
        copy.wait()
    steps = hidden.shape[1] // tile
    slots = ready.shape[0]

    def copy_out(i):
        return pltpu.make_async_copy(
            ready.at[i % slots], out_ref.at[pl.ds(i * tile, tile)], sems.at[i % slots]
        )

    for i in range(steps):
        if i >= slots:
            copy_out(i - slots).wait()
        ready[i % slots] = lax.dot_general(
            hidden[:, i * tile : (i + 1) * tile],
            grads[...],
            (((0,), (0,)), ((), ())),
            preferred_element_type=F32,
        ).astype(BF16)
        copy_out(i).start()
    for i in range(steps - slots, steps):
        copy_out(i).wait()


def outer(shift, grads, hidden, tile=128, slots=26):
    tok, width = hidden[0].shape[0] // 2, grads[0].shape[1]
    rows = hidden[0].shape[1]
    return pl.pallas_call(
        functools.partial(outer_kernel, tok, tile),
        out_shape=[
            jax.ShapeDtypeStruct((rows, width), BF16),
            jax.ShapeDtypeStruct((8, 128), F32),
        ],
        in_specs=[SMEM] + [ANYWHERE] * 8,
        out_specs=[ANYWHERE, VMEM],
        scratch_shapes=[
            pltpu.VMEM((8 * tok, width), BF16),
            pltpu.VMEM((8 * tok, rows), BF16),
            pltpu.VMEM((slots, tile, width), BF16),
            pltpu.SemaphoreType.DMA((slots,)),
            pltpu.SemaphoreType.DMA((2, 8)),
        ],
        compiler_params=pltpu.CompilerParams(vmem_limit_bytes=40 << 20),
        cost_estimate=QUICK,
    )(shift, *in_hbm([*grads, *hidden]))


def finish(hidden_grad, gate_vals, up_vals):
    sigma_gate = jax.nn.sigmoid(gate_vals)
    up_grad = (hidden_grad * (gate_vals * sigma_gate)).astype(BF16)
    gate_grad = (
        hidden_grad * up_vals * sigma_gate * (1.0 + gate_vals * (1.0 - sigma_gate))
    ).astype(BF16)
    return gate_grad, up_grad


def finish_kernel(parts, gate_ref, up_ref, *refs):
    gate_out, up_out = refs[-2:]
    at = 0
    for i in range(parts):
        p0, r1, r2, r3 = refs[4 * i : 4 * i + 4]
        columns = slice(at, at + p0.shape[1])
        total = p0[...] + r1[...].astype(F32) + r2[...].astype(F32) + r3[...].astype(F32)
        gate_out[:, columns], up_out[:, columns] = finish(
            total, gate_ref[:, columns].astype(F32), up_ref[:, columns].astype(F32)
        )
        at += p0.shape[1]


def finished(gate_pre, up_pre, parts, after):
    terms = [term for part in parts for term in part]
    return pl.pallas_call(
        functools.partial(finish_kernel, len(parts)),
        out_shape=[jax.ShapeDtypeStruct(gate_pre.shape, BF16)] * 2,
        in_specs=[VMEM] * (2 + len(terms)) + [ANYWHERE],
        out_specs=[VMEM] * 2,
        compiler_params=pltpu.CompilerParams(vmem_limit_bytes=16 << 20),
        cost_estimate=QUICK,
    )(gate_pre, up_pre, *terms, after)


def by_distance(gate_pre, up_pre, out_grad, down_weight):
    ff = gate_pre.shape[1]
    half = ff // 2
    row, col, depth = (lax.axis_index(a) for a in ("row", "col", "depth"))
    shift = jnp.bitwise_xor(row, col).astype(jnp.int32).reshape(1)

    def send(x, axis, distance):
        return lax.ppermute(x, axis, xor_pairs(lax.axis_size(axis), distance))

    mine, theirs, g0 = hidden_halves(
        depth.astype(jnp.int32).reshape(1), gate_pre, up_pre, out_grad
    )
    other = send(theirs, "depth", 1)
    g2 = send(g0, "row", 2)
    pair, h0 = stacked(g0, g2, mine, other)
    cores = send(pair, "row", 1)
    h2 = send(h0, "col", 2)
    h1 = send(h0, "col", 1)
    other_pair = send(pair, "depth", 1)

    def reduced(terms):
        p0, p1, p2, p3 = terms
        r2, r3, r1 = send(p2, "col", 2), send(p3, "col", 3), send(p1, "col", 1)
        return p0, r1, r2, r3

    most = half // 256 * 256
    terms = partials(shift, (pair, cores), down_weight, 0, most)
    first = reduced(terms)
    h2, _ = lax.optimization_barrier((h2, terms[0]))
    other_pair, _ = lax.optimization_barrier((other_pair, terms[0]))
    h3 = send(h2, "col", 1)
    other_cores = send(other_pair, "row", 1)
    other_cores, shift, _ = lax.optimization_barrier((other_cores, shift, terms[0]))
    second = reduced(partials(shift, (pair, cores), down_weight, most, ff - most))
    shift, *first = lax.optimization_barrier((shift, *first))
    weight_grad, token = outer(
        shift, (pair, cores, other_pair, other_cores), (h0, h2, h1, h3)
    )
    gate_grad, up_grad = finished(gate_pre, up_pre, (first, second), token)
    return weight_grad, gate_grad, up_grad


def by_collectives(gate_pre, up_pre, out_grad, down_weight):
    tok, ff = gate_pre.shape
    n_row, n_depth = lax.axis_size("row"), lax.axis_size("depth")
    gate_vals = gate_pre.astype(F32)
    up_vals = up_pre.astype(F32)
    hidden = (gate_vals * jax.nn.sigmoid(gate_vals) * up_vals).astype(BF16)
    layers = lax.all_to_all(hidden, "depth", split_axis=1, concat_axis=0, tiled=True)
    hidden_all = lax.all_gather(layers, "col", axis=0, tiled=True)
    grads_all = lax.all_gather(out_grad, ("row", "depth"), axis=0, tiled=True)
    weight_grad = lax.dot_general(
        hidden_all, grads_all, (((0,), (0,)), ((), ())), preferred_element_type=F32
    ).astype(BF16)
    layer = lax.dynamic_index_in_dim(
        grads_all.reshape(n_row, n_depth, tok, -1), lax.axis_index("depth"), 1, False
    ).reshape(n_row * tok, -1)
    hidden_terms = lax.dot_general(
        layer, down_weight, (((1,), (1,)), ((), ())), preferred_element_type=F32
    )
    hidden_grad = lax.psum_scatter(hidden_terms, "col", scatter_dimension=0, tiled=True)
    gate_grad, up_grad = finish(hidden_grad, gate_vals, up_vals)
    return weight_grad, gate_grad, up_grad


def solution(mesh):
    sizes = tuple(mesh.shape[a] for a in ("row", "col", "depth"))
    placed = (
        P(("col", "depth"), "row"),
        P(("col", "depth"), "row"),
        P(("row", "depth"), "col"),
        P("row", "col"),
    )
    return jax.shard_map(
        by_distance if sizes == (4, 4, 2) else by_collectives,
        mesh=mesh,
        in_specs=placed,
        out_specs=(
            P(("row", "depth"), "col"),
            P(("col", "depth"), "row"),
            P(("col", "depth"), "row"),
        ),
        check_vma=False,
    )
```

```python
import functools

import jax
import jax.numpy as jnp
from jax import lax
from jax.experimental import pallas as pl
from jax.experimental.pallas import tpu as pltpu
from jax.sharding import PartitionSpec as P

BF16 = jnp.bfloat16
QUICK = pl.CostEstimate(flops=1, bytes_accessed=1, transcendentals=0)
F32 = jnp.float32


def xor_pairs(size, distance):
    return [(i, i ^ distance) for i in range(size)]


def block_copies(shift, refs, scratch, base, tok, sems):
    copies = []
    for i, (value, ref) in enumerate(zip((0, 2, 1, 3), refs)):
        start = pl.multiple_of(base + jnp.bitwise_xor(shift, value) * tok, tok)
        copies.append(
            pltpu.make_async_copy(ref, scratch.at[pl.ds(start, tok)], sems.at[i])
        )
    return copies


def hidden_kernel(depth_ref, gate_ref, up_ref, mine, theirs):
    half = mine.shape[1]
    for ref, at in ((mine, depth_ref[0]), (theirs, 1 - depth_ref[0])):
        columns = pl.ds(pl.multiple_of(at * half, 128), half)
        gate = gate_ref[:, columns].astype(F32)
        up = up_ref[:, columns].astype(F32)
        ref[...] = (gate * jax.nn.sigmoid(gate) * up).astype(ref.dtype)


def hidden_halves(depth, gate_pre, up_pre):
    tok, ff = gate_pre.shape
    vmem = pl.BlockSpec(memory_space=pltpu.VMEM)
    return pl.pallas_call(
        hidden_kernel,
        out_shape=[jax.ShapeDtypeStruct((tok, ff // 2), BF16)] * 2,
        in_specs=[pl.BlockSpec(memory_space=pltpu.SMEM), vmem, vmem],
        out_specs=[vmem, vmem],
        compiler_params=pltpu.CompilerParams(vmem_limit_bytes=8 << 20),
        cost_estimate=QUICK,
    )(depth, gate_pre, up_pre)


def cuts(rows, most):
    parts = -(-rows // most)
    step = -(-rows // parts // 128) * 128
    return [(at, min(step, rows - at)) for at in range(0, rows, step)]


def in_hbm(arrays):
    return [pltpu.with_memory_space_constraint(x, pltpu.HBM) for x in arrays]


ANYWHERE = pl.BlockSpec(memory_space=pl.ANY)
VMEM = pl.BlockSpec(memory_space=pltpu.VMEM)
SMEM = pl.BlockSpec(memory_space=pltpu.SMEM)


def partial_kernel(tok, first, tiles, n_after, shift_ref, *refs):
    grads_in, w_ref, refs = refs[:4], refs[4], refs[5 + n_after :]
    terms_out, (grads, rows, sems, w_sems) = refs[:4], refs[4:]
    copies = block_copies(shift_ref[0], grads_in, grads, 0, tok, sems)
    fetches = [
        pltpu.make_async_copy(
            w_ref.at[pl.ds(first + at, size)], rows.at[pl.ds(at, size)], w_sems.at[i]
        )
        for i, (at, size) in enumerate(tiles)
    ]
    for copy in copies + fetches[:1]:
        copy.start()
    for copy in copies:
        copy.wait()
    for fetch in fetches[1:]:
        fetch.start()
    for fetch, (at, size) in zip(fetches, tiles):
        fetch.wait()
        terms = lax.dot_general(
            grads[...],
            rows[at : at + size, :],
            (((1,), (1,)), ((), ())),
            preferred_element_type=F32,
        )
        for k, ref in enumerate(terms_out):
            ref[:, at : at + size] = terms[k * tok : (k + 1) * tok].astype(ref.dtype)


def partials(shift, grads, weight, first, rows, after):
    tok, width = grads[0].shape
    tiles = [(0, 256)] + [(256 + at, size) for at, size in cuts(rows - 256, 512)]
    return pl.pallas_call(
        functools.partial(partial_kernel, tok, first, tiles, len(after)),
        out_shape=[jax.ShapeDtypeStruct((tok, rows), F32)]
        + [jax.ShapeDtypeStruct((tok, rows), BF16)] * 3,
        in_specs=[SMEM] + [ANYWHERE] * (5 + len(after)),
        out_specs=[VMEM] * 4,
        scratch_shapes=[
            pltpu.VMEM((4 * tok, width), BF16),
            pltpu.VMEM((rows, width), BF16),
            pltpu.SemaphoreType.DMA((4,)),
            pltpu.SemaphoreType.DMA((len(tiles),)),
        ],
        compiler_params=pltpu.CompilerParams(vmem_limit_bytes=40 << 20),
        cost_estimate=QUICK,
    )(shift, *grads, *in_hbm([weight, *after]))


def outer_kernel(tok, tile, shift_ref, *refs):
    out_ref, token, grads, hidden, ready, sems, in_sems = refs[17:]
    token[...] = jnp.zeros_like(token)
    copies = []
    for half in range(2):
        base = 4 * tok * half
        copies += block_copies(
            shift_ref[0], refs[4 * half : 4 * half + 4], grads, base, tok, in_sems.at[half]
        )
        for k, ref in zip((0, 2, 1, 3), refs[8 + 4 * half : 12 + 4 * half]):
            rows = pl.ds(base + k * tok, tok)
            copies.append(
                pltpu.make_async_copy(ref, hidden.at[rows], in_sems.at[half, 4 + k])
            )
    for copy in copies:
        copy.start()
    for copy in copies:
        copy.wait()
    steps = hidden.shape[1] // tile
    slots = ready.shape[0]

    def copy_out(i):
        return pltpu.make_async_copy(
            ready.at[i % slots], out_ref.at[pl.ds(i * tile, tile)], sems.at[i % slots]
        )

    for i in range(steps):
        if i >= slots:
            copy_out(i - slots).wait()
        ready[i % slots] = lax.dot_general(
            hidden[:, i * tile : (i + 1) * tile],
            grads[...],
            (((0,), (0,)), ((), ())),
            preferred_element_type=F32,
        ).astype(BF16)
        copy_out(i).start()
    for i in range(steps - slots, steps):
        copy_out(i).wait()


def outer(shift, grads, hidden, after, tile=128, slots=26):
    tok, width = grads[0].shape
    rows = hidden[0].shape[1]
    return pl.pallas_call(
        functools.partial(outer_kernel, tok, tile),
        out_shape=[
            jax.ShapeDtypeStruct((rows, width), BF16),
            jax.ShapeDtypeStruct((8, 128), F32),
        ],
        in_specs=[SMEM] + [ANYWHERE] * 17,
        out_specs=[ANYWHERE, VMEM],
        scratch_shapes=[
            pltpu.VMEM((8 * tok, width), BF16),
            pltpu.VMEM((8 * tok, rows), BF16),
            pltpu.VMEM((slots, tile, width), BF16),
            pltpu.SemaphoreType.DMA((slots,)),
            pltpu.SemaphoreType.DMA((2, 8)),
        ],
        compiler_params=pltpu.CompilerParams(vmem_limit_bytes=40 << 20),
        cost_estimate=QUICK,
    )(shift, *in_hbm([*grads, *hidden]), after)


def finish(hidden_grad, gate_vals, up_vals):
    sigma_gate = jax.nn.sigmoid(gate_vals)
    up_grad = (hidden_grad * (gate_vals * sigma_gate)).astype(BF16)
    gate_grad = (
        hidden_grad * up_vals * sigma_gate * (1.0 + gate_vals * (1.0 - sigma_gate))
    ).astype(BF16)
    return gate_grad, up_grad


def finish_kernel(gate_ref, up_ref, p0, r1, r2, r3, *refs):
    gate_out, up_out, token = refs[-3:]
    total = p0[...] + r1[...].astype(F32) + r2[...].astype(F32) + r3[...].astype(F32)
    gate_out[...], up_out[...] = finish(
        total, gate_ref[...].astype(F32), up_ref[...].astype(F32)
    )
    token[...] = jnp.zeros_like(token)


def finished(gate_pre, up_pre, part, terms, others):
    tok, width = terms[0].shape
    here = pl.BlockSpec((tok, width), lambda i: (0, part))
    term = pl.BlockSpec((tok, width), lambda i: (0, 0))
    return pl.pallas_call(
        finish_kernel,
        grid=(1,),
        out_shape=[jax.ShapeDtypeStruct(gate_pre.shape, BF16)] * 2
        + [jax.ShapeDtypeStruct((8, 128), F32)],
        in_specs=[here, here] + [term] * 4 + [ANYWHERE] * len(others),
        out_specs=[here, here, pl.BlockSpec((8, 128), lambda i: (0, 0))],
        input_output_aliases={6: 0, 7: 1} if part else {},
        compiler_params=pltpu.CompilerParams(vmem_limit_bytes=16 << 20),
        cost_estimate=QUICK,
    )(gate_pre, up_pre, *terms, *others)


def by_distance(gate_pre, up_pre, out_grad, down_weight):
    ff = gate_pre.shape[1]
    half = ff // 2
    row, col, depth = (lax.axis_index(a) for a in ("row", "col", "depth"))
    shift = jnp.bitwise_xor(row, col).astype(jnp.int32).reshape(1)

    def send(x, axis, distance):
        return lax.ppermute(x, axis, xor_pairs(lax.axis_size(axis), distance))

    g0 = out_grad
    g2 = send(g0, "row", 2)
    g1 = send(g0, "row", 1)
    g3 = send(g2, "row", 1)

    mine, theirs = hidden_halves(depth.astype(jnp.int32).reshape(1), gate_pre, up_pre)
    other = send(theirs, "depth", 1)

    def gather_col(x):
        x2 = send(x, "col", 2)
        return x, x2, send(x, "col", 1), send(x2, "col", 1)

    own_layer = gather_col(mine)
    other_layer = gather_col(other)

    q0 = send(g0, "depth", 1)
    q2 = send(q0, "row", 2)
    q1 = send(q0, "row", 1)
    q3 = send(q2, "row", 1)

    grads = (g0, g2, g1, g3)
    def reduced(terms):
        p0, p1, p2, p3 = terms
        r2, r3, r1 = send(p2, "col", 2), send(p3, "col", 3), send(p1, "col", 1)
        return p0, r1, r2, r3

    terms = partials(shift, grads, down_weight, 0, half, (other,))
    first = reduced(terms)
    second = reduced(partials(shift, grads, down_weight, half, half, (terms[0], *own_layer[1:3], *other_layer[1:3], q0)))
    gate_grad, up_grad, token = finished(gate_pre, up_pre, 0, first, ())
    weight_grad, token = outer(
        shift,
        (g0, g2, g1, g3, q0, q2, q1, q3),
        own_layer + other_layer,
        token,
    )
    gate_grad, up_grad, _ = finished(
        gate_pre, up_pre, 1, second, (gate_grad, up_grad, token)
    )
    return weight_grad, gate_grad, up_grad


def by_collectives(gate_pre, up_pre, out_grad, down_weight):
    tok, ff = gate_pre.shape
    n_row, n_depth = lax.axis_size("row"), lax.axis_size("depth")
    gate_vals = gate_pre.astype(F32)
    up_vals = up_pre.astype(F32)
    hidden = (gate_vals * jax.nn.sigmoid(gate_vals) * up_vals).astype(BF16)
    layers = lax.all_to_all(hidden, "depth", split_axis=1, concat_axis=0, tiled=True)
    hidden_all = lax.all_gather(layers, "col", axis=0, tiled=True)
    grads_all = lax.all_gather(out_grad, ("row", "depth"), axis=0, tiled=True)
    weight_grad = lax.dot_general(
        hidden_all, grads_all, (((0,), (0,)), ((), ())), preferred_element_type=F32
    ).astype(BF16)
    layer = lax.dynamic_index_in_dim(
        grads_all.reshape(n_row, n_depth, tok, -1), lax.axis_index("depth"), 1, False
    ).reshape(n_row * tok, -1)
    hidden_terms = lax.dot_general(
        layer, down_weight, (((1,), (1,)), ((), ())), preferred_element_type=F32
    )
    hidden_grad = lax.psum_scatter(hidden_terms, "col", scatter_dimension=0, tiled=True)
    gate_grad, up_grad = finish(hidden_grad, gate_vals, up_vals)
    return weight_grad, gate_grad, up_grad


def solution(mesh):
    sizes = tuple(mesh.shape[a] for a in ("row", "col", "depth"))
    placed = (
        P(("col", "depth"), "row"),
        P(("col", "depth"), "row"),
        P(("row", "depth"), "col"),
        P("row", "col"),
    )
    return jax.shard_map(
        by_distance if sizes == (4, 4, 2) else by_collectives,
        mesh=mesh,
        in_specs=placed,
        out_specs=(
            P(("row", "depth"), "col"),
            P(("col", "depth"), "row"),
            P(("col", "depth"), "row"),
        ),
        check_vma=False,
    )
```
